32 devices in a mesh: dp: 4 (over y, x), mp: 8 (over z, core).
Axes of the slice: x: 2, y: 2, z: 4, core: 2. Of those that a mesh axis runs over, the one named last changes fastest.
Arguments:
- activations: bfloat16 [1024, 8192], P(('dp', 'mp')), may hold values from -6 to 6
- out_grads: bfloat16 [1024, 14336], P('dp', 'mp'), may hold values from -0.75 to 0.75
- basis: bfloat16 [8192, 512], P('mp'), may hold values from -0.0625 to 0.0625
- first_moment: float32 [512, 14336], P(None, 'mp'), may hold values from -3 to 3
- second_moment: float32 [512, 14336], P(None, 'mp'), may hold values from 0.0001 to 0.01
Outputs:
- update: bfloat16 [8192, 14336], P(None, 'mp')
- new_first: float32 [512, 14336], P(None, 'mp')
- new_second: float32 [512, 14336], P(None, 'mp')
The draws below stay inside these ranges and needn't reach their ends.
All inputs are finite; a program needn't handle non-finite values.
Results may differ from the reference program's by a relative error of at most 0.0051.
Values may be sent and summed in bfloat16 or wider, within the bound.
A program may use at most 128 MiB of HBM per device.

```python
import math
import jax
import jax.numpy as jnp
from jax import lax

D = 8192
FF = 14336
RANK = 512
STEP = 10
TOKENS = 1024
N_DP = 4


def steps_of(own_key, dims, cuts, smallest, top_value):
    factor_of, own = 1.0, jax.random.fold_in(own_key, 6)
    for position, shards_of in cuts:
        draws = jnp.exp(jax.random.uniform(jax.random.fold_in(own, position), (shards_of,), jnp.float32, smallest / len(cuts), top_value / len(cuts)))
        factor_of = factor_of * jnp.repeat(draws, dims[position] // shards_of).reshape([-1 if axis == position else 1 for axis in range(len(dims))])
    return factor_of


def scatter_about(stream_key, dims, scale, reach, split=(), kind=jnp.bfloat16):
    entries = scale * jax.random.normal(stream_key, dims, jnp.float32)
    if split:
        entries = entries * steps_of(stream_key, dims, split, -0.22, 0.18)
    return jnp.clip(entries, -reach, reach).astype(kind)


def setup_inputs(seed: int = 0) -> dict:
    key_of = jax.random.split(jax.random.key(seed), 6)
    activations = scatter_about(key_of[0], (TOKENS, D), 1.0, 6.0, ((0, 32),))
    out_grads = scatter_about(key_of[1], (TOKENS, FF), 0.125, 0.75, ((0, 4), (1, 8)))
    basis = scatter_about(key_of[2], (D, RANK), D ** -0.5, 0.0625, ((0, 8),))
    first_moment = scatter_about(key_of[3], (RANK, FF), 0.5, 3.0, ((1, 8),), jnp.float32)
    second_moment = jnp.clip(jnp.exp(math.log(0.01) - 4.6051702 * jax.random.uniform(key_of[4], (RANK, FF), jnp.float32) ** steps_of(key_of[4], (RANK, FF), ((1, 8),), -0.2, 0.2)), 0.0001, 0.01)
    return {"activations": activations, "out_grads": out_grads, "basis": basis, "first_moment": first_moment, "second_moment": second_moment}


def reference(activations, out_grads, basis, first_moment, second_moment):
    basis_wide = basis.astype(jnp.float32)
    reduced = jnp.dot(activations.astype(jnp.float32), basis_wide, precision=lax.Precision.HIGHEST)
    projected = jnp.dot(reduced.T, out_grads.astype(jnp.float32), precision=lax.Precision.HIGHEST) / N_DP
    new_first = 0.9 * first_moment + 0.1 * projected
    new_second = 0.999 * second_moment + 0.001 * projected * projected
    first_hat = new_first / (1.0 - 0.9 ** STEP)
    second_hat = new_second / (1.0 - 0.999 ** STEP)
    normalized = (first_hat / (jnp.sqrt(second_hat) + 1e-08)).astype(jnp.bfloat16)
    update = jnp.dot(basis_wide, normalized.astype(jnp.float32), precision=lax.Precision.HIGHEST).astype(jnp.bfloat16)
    return (update, new_first, new_second)
```

```python
import functools
import itertools

import jax
import jax.numpy as jnp
from jax import lax
from jax.experimental import pallas as pl
from jax.experimental.pallas import tpu as pltpu
from jax.sharding import PartitionSpec as P

STEP = 10
MESH = pl.DeviceIdType.MESH


def flip(index, stride):
    return index + stride - 2 * stride * lax.rem(lax.div(index, stride), 2)


def count_of(n_dp, n_mp):
    chips = n_mp // 2
    both = 2 * (n_dp - 1)
    return (chips - 1) * (2 + both) + 1 + both + (n_mp - 1) + both + (n_dp - 1)


def gather_kernel(
    n_dp, n_mp, act_ref, og_ref, basis_ref, basis_out, og_out, red_out,
    bas, og, red, acc, send, recv, local,
):
    q, m = lax.axis_index("dp"), lax.axis_index("mp")
    chips = n_mp // 2
    z, c = lax.div(m, 2), lax.rem(m, 2)
    twin = (q, 2 * z + 1 - c)
    strides = [1 << s for s in range(n_dp.bit_length() - 1)]
    orders = [strides, strides[::-1]]
    rows = basis_ref.shape[0]
    piece = rows // n_dp
    tokens = og_ref.shape[0]
    mine = act_ref.shape[0]

    barrier = pltpu.get_barrier_semaphore()
    for k in range(1, n_mp):
        pl.semaphore_signal(barrier, inc=1, device_id=(q, lax.rem(m + k, n_mp)), device_id_type=MESH)
    for stride in strides:
        pl.semaphore_signal(barrier, inc=1, device_id=(flip(q, stride), m), device_id_type=MESH)
    pl.semaphore_wait(barrier, n_mp - 1 + len(strides))

    numbers = itertools.count()
    sent = []

    def push(src, dst, device):
        i = next(numbers)
        copy = pltpu.make_async_remote_copy(
            src_ref=src, dst_ref=dst, send_sem=send.at[i], recv_sem=recv.at[i],
            device_id=device, device_id_type=MESH,
        )
        copy.start()
        sent.append(copy)
        return copy

    def part(ref, start, size):
        return ref.at[pl.ds(pl.multiple_of(start, 16), size), :]

    def stage(ref, base, step, size, half, held, s):
        stride = orders[half][s]
        partner = (flip(q, stride), m)
        copies = []
        for b in held:
            where = part(ref, base + b * step + half * size, size)
            copies.append(push(where, where, partner))
        return copies, held + [flip(b, stride) for b in held]

    def shard(k, core):
        return (2 * lax.rem(z - k + chips, chips) + core) * rows

    own = m * rows
    z_copies = []
    for k in range(1, chips):
        z_copies.append(push(
            part(basis_ref, q * piece, piece), part(bas, own + q * piece, piece),
            (q, 2 * lax.rem(z + k, chips) + c),
        ))
    twin_own = push(basis_ref, part(bas, own, rows), twin)

    og_half = tokens // 2
    og_held, og_copies = [[q], [q]], [[], []]
    for h in range(2):
        stride = orders[h][0]
        og_copies[h].append(push(
            part(og_ref, h * og_half, og_half), part(og, q * tokens + h * og_half, og_half),
            (flip(q, stride), m),
        ))
        og_held[h] = [q, flip(q, stride)]
    own_basis = pltpu.make_async_copy(basis_ref, part(bas, own, rows), local.at[0])
    own_basis.start()
    own_og = pltpu.make_async_copy(og_ref, part(og, q * tokens, tokens), local.at[1])
    own_og.start()

    def add(start):
        where = pl.multiple_of(start, 128)
        acc[...] += jnp.dot(
            act_ref[:, pl.ds(where, rows)], bas[pl.ds(where, rows), :],
            preferred_element_type=jnp.float32,
        )

    acc[...] = jnp.zeros_like(acc)
    own_basis.wait()
    add(own)

    half = piece // 2
    held = [[[q], [q]] for _ in range(chips)]
    flying = [[[], []] for _ in range(chips)]
    for s in range(len(strides)):
        for k in range(1, chips):
            base = shard(k, c)
            if s == 0:
                z_copies[k - 1].wait_recv()
            for h in range(2):
                for copy in flying[k][h]:
                    copy.wait_recv()
                flying[k][h], held[k][h] = stage(bas, base, piece, half, h, held[k][h], s)
    own_og.wait()
    for s in range(1, len(strides)):
        for h in range(2):
            for copy in og_copies[h]:
                copy.wait_recv()
            og_copies[h], og_held[h] = stage(og, 0, tokens, og_half, h, og_held[h], s)

    twin_own.wait_recv()
    add((2 * z + 1 - c) * rows)
    twin_copies = []
    for k in range(1, chips):
        base = shard(k, c)
        for h in range(2):
            for copy in flying[k][h]:
                copy.wait_recv()
        where = part(bas, base, rows)
        twin_copies.append(push(where, where, twin))
        add(base)
    for k in range(1, chips):
        twin_copies[k - 1].wait_recv()
        add(shard(k, 1 - c))

    place = q * tokens + m * mine
    red[pl.ds(pl.multiple_of(place, 16), mine), :] = acc[...].astype(red.dtype)
    group_copies = []
    for k in range(1, n_mp):
        where = part(red, place, mine)
        group_copies.append(push(where, where, (q, lax.rem(m + k, n_mp))))
    out_basis = pltpu.make_async_copy(bas, basis_out, local.at[2])
    out_basis.start()
    for copy in group_copies:
        copy.wait_recv()
    quarter = tokens // 4
    side = c * (tokens // 2)
    red_held, red_copies = [[q], [q]], [[], []]
    for s in range(len(strides)):
        for h in range(2):
            for copy in red_copies[h]:
                copy.wait_recv()
            red_copies[h], red_held[h] = stage(red, side, tokens, quarter, h, red_held[h], s)
    for h in range(2):
        for copy in red_copies[h]:
            copy.wait_recv()
    last = []
    for k in range(1, n_dp):
        where = part(red, lax.rem(q + k, n_dp) * tokens + side, tokens // 2)
        last.append(push(where, where, twin))
    for h in range(2):
        for copy in og_copies[h]:
            copy.wait_recv()
    out_og = pltpu.make_async_copy(og, og_out, local.at[3])
    out_og.start()
    for copy in last:
        copy.wait_recv()
    out_red = pltpu.make_async_copy(red, red_out, local.at[4])
    out_red.start()
    for copy in sent:
        copy.wait_send()
    out_basis.wait()
    out_og.wait()
    out_red.wait()


def gather(activations, out_grads, basis):
    n_dp, n_mp = lax.axis_size("dp"), lax.axis_size("mp")
    mine, width = activations.shape
    tokens, columns = out_grads.shape
    rank = basis.shape[1]
    count = count_of(n_dp, n_mp)
    anywhere = pl.BlockSpec(memory_space=pl.ANY)
    shapes = [(width, rank), (n_dp * tokens, columns), (n_dp * tokens, rank)]
    return pl.pallas_call(
        functools.partial(gather_kernel, n_dp, n_mp),
        out_shape=[jax.ShapeDtypeStruct(shape, jnp.bfloat16) for shape in shapes],
        in_specs=[pl.BlockSpec(memory_space=pltpu.VMEM), anywhere, anywhere],
        out_specs=[anywhere] * 3,
        scratch_shapes=[pltpu.VMEM(shape, jnp.bfloat16) for shape in shapes]
        + [
            pltpu.VMEM((mine, rank), jnp.float32),
            pltpu.SemaphoreType.DMA((count,)),
            pltpu.SemaphoreType.DMA((count,)),
            pltpu.SemaphoreType.DMA((5,)),
        ],
        compiler_params=pltpu.CompilerParams(
            collective_id=0, has_side_effects=True, vmem_limit_bytes=40 * 2**20
        ),
        name="gather",
    )(activations, out_grads, basis)


def step_kernel(
    groups, basis_ref, red_ref, og_ref, first_ref, second_ref, update_ref, new_first_ref,
    new_second_ref, turned,
):
    @pl.when(pl.program_id(0) == 0)
    def _():
        turned[...] = red_ref[...].T

    projected = jnp.dot(turned[...], og_ref[...], preferred_element_type=jnp.float32) / groups
    new_first = 0.9 * first_ref[...] + 0.1 * projected
    new_second = 0.999 * second_ref[...] + 0.001 * projected * projected
    new_first_ref[...] = new_first
    new_second_ref[...] = new_second
    first_hat = new_first / (1.0 - 0.9**STEP)
    second_hat = new_second / (1.0 - 0.999**STEP)
    normalized = (first_hat / (jnp.sqrt(second_hat) + 1e-08)).astype(jnp.bfloat16)
    rows = basis_ref.shape[0]
    chunk = min(rows, 1024)

    def one(i, carry):
        where = pl.ds(pl.multiple_of(i * chunk, chunk), chunk)
        update_ref[where, :] = jnp.dot(
            basis_ref[where, :], normalized, preferred_element_type=jnp.float32
        ).astype(update_ref.dtype)
        return carry

    lax.fori_loop(0, rows // chunk, one, 0)


def step(basis, red, og, first, second, groups):
    rank, columns = first.shape
    width, tokens = basis.shape[0], og.shape[0]
    block = 256 if columns % 256 == 0 else 128
    whole = lambda shape: pl.BlockSpec(shape, lambda j: (0, 0), pipeline_mode=pl.Buffered(1))
    column = lambda n: pl.BlockSpec((n, block), lambda j: (0, j))
    return pl.pallas_call(
        functools.partial(step_kernel, groups),
        grid=(columns // block,),
        out_shape=[
            jax.ShapeDtypeStruct((width, columns), jnp.bfloat16),
            jax.ShapeDtypeStruct(first.shape, jnp.float32),
            jax.ShapeDtypeStruct(second.shape, jnp.float32),
        ],
        in_specs=[
            whole((width, rank)), whole((tokens, rank)), column(tokens), column(rank), column(rank)
        ],
        out_specs=[column(width), column(rank), column(rank)],
        scratch_shapes=[pltpu.VMEM((rank, tokens), jnp.bfloat16)],
        compiler_params=pltpu.CompilerParams(vmem_limit_bytes=48 * 2**20),
        name="step",
    )(basis, red, og, first, second)


def body(activations, out_grads, basis, first_moment, second_moment):
    whole_basis, whole_grads, reduced = gather(activations, out_grads, basis)
    return tuple(step(
        whole_basis, reduced, whole_grads, first_moment, second_moment, lax.axis_size("dp")
    ))


def solution(mesh):
    return jax.shard_map(
        body,
        mesh=mesh,
        in_specs=(
            P(("dp", "mp"), None),
            P("dp", "mp"),
            P("mp", None),
            P(None, "mp"),
            P(None, "mp"),
        ),
        out_specs=(P(None, "mp"), P(None, "mp"), P(None, "mp")),
        check_vma=False,
    )
```

```python
import functools
import itertools

import jax
import jax.numpy as jnp
from jax import lax
from jax.experimental import pallas as pl
from jax.experimental.pallas import tpu as pltpu
from jax.sharding import PartitionSpec as P

STEP = 10
MESH = pl.DeviceIdType.MESH


def flip(index, stride):
    return index + stride - 2 * stride * lax.rem(lax.div(index, stride), 2)


def counts_of(n_dp, n_mp):
    hops = 4 * (n_mp // 2 - 1)
    both = 2 * (n_dp - 1)
    return hops, 1 + both + (n_mp - 1) + both + (n_dp - 1)


def gather_kernel(
    n_dp, n_mp, act_ref, og_ref, basis_ref, basis_out, og_out, red_out,
    act, bas, og, red, acc, send, recv, hop_send, hop_recv, local,
):
    q, m = lax.axis_index("dp"), lax.axis_index("mp")
    chips = n_mp // 2
    z, c = lax.div(m, 2), lax.rem(m, 2)
    twin = (q, 2 * z + 1 - c)
    strides = [1 << s for s in range(n_dp.bit_length() - 1)]
    orders = [strides, strides[::-1]]
    rows = basis_ref.shape[0]
    piece = rows // 4
    tokens = og_ref.shape[0]
    mine = act_ref.shape[0]

    load_act = pltpu.make_async_copy(act_ref, act, local.at[5])
    load_act.start()
    own_basis = pltpu.make_async_copy(basis_ref, bas.at[pl.ds(pl.multiple_of(m * rows, 128), rows), :], local.at[0])
    own_basis.start()
    own_og = pltpu.make_async_copy(og_ref, og.at[pl.ds(pl.multiple_of(q * tokens, 128), tokens), :], local.at[1])
    own_og.start()

    barrier = pltpu.get_barrier_semaphore()
    for k in range(1, n_mp):
        pl.semaphore_signal(barrier, inc=1, device_id=(q, lax.rem(m + k, n_mp)), device_id_type=MESH)
    for stride in strides:
        pl.semaphore_signal(barrier, inc=1, device_id=(flip(q, stride), m), device_id_type=MESH)
    pl.semaphore_wait(barrier, n_mp - 1 + len(strides))

    numbers = itertools.count()
    sent = []

    def push(src, dst, device):
        i = next(numbers)
        copy = pltpu.make_async_remote_copy(
            src_ref=src, dst_ref=dst, send_sem=send.at[i], recv_sem=recv.at[i],
            device_id=device, device_id_type=MESH,
        )
        copy.start()
        sent.append(copy)
        return copy

    def part(ref, start, size):
        return ref.at[pl.ds(pl.multiple_of(start, 16), size), :]

    def stage(ref, base, step, size, half, held, s):
        stride = orders[half][s]
        partner = (flip(q, stride), m)
        copies = []
        for b in held:
            where = part(ref, base + b * step + half * size, size)
            copies.append(push(where, where, partner))
        return copies, held + [flip(b, stride) for b in held]

    parity = lax.rem(lax.rem(q, 2) + lax.rem(lax.div(q, 2), 2), 2)
    neighbours = [(flip(q, 1), m), (flip(q, 2), m)]
    ways = [1, -1]

    def hop(kind, way, t, j, shard_z, half_number, device):
        i = (way * (chips - 1) + t) * 2 + j
        where = part(bas, (2 * shard_z + c) * rows + half_number * 2 * piece + j * piece, piece)
        return pltpu.make_async_remote_copy(
            src_ref=where, dst_ref=where, send_sem=hop_send.at[kind, i],
            recv_sem=hop_recv.at[kind, i], device_id=device, device_id_type=MESH,
        )

    def gives(way, t):
        if way == 0:
            return jnp.logical_and(z < chips - 1, z - t >= 0), z - t
        return jnp.logical_and(z > 0, z + t <= chips - 1), z + t

    def gets(way, t):
        if way == 0:
            return z - 1 - t >= 0, z - 1 - t
        return z + 1 + t <= chips - 1, z + 1 + t

    def along(way, t, j):
        return hop(0, way, t, j, gives(way, t)[1], parity, (q, m + 2 * ways[way]))

    def along_in(way, t, j):
        return hop(0, way, t, j, gets(way, t)[1], parity, (q, m - 2 * ways[way]))

    def across(way, t, j):
        return hop(1, way, t, j, gets(way, t)[1], parity, neighbours[j])

    def across_in(way, t, j):
        return hop(1, way, t, j, gets(way, t)[1], 1 - parity, neighbours[j])

    def over(kind, way, t, j):
        half_number = parity if kind == 2 else 1 - parity
        return hop(kind, way, t, j, gets(way, t)[1], half_number, twin)

    def over_in(kind, way, t, j):
        half_number = parity if kind == 2 else 1 - parity
        i = (way * (chips - 1) + t) * 2 + j
        start = (2 * gets(way, t)[1] + 1 - c) * rows + half_number * 2 * piece + j * piece
        where = part(bas, start, piece)
        return pltpu.make_async_remote_copy(
            src_ref=where, dst_ref=where, send_sem=hop_send.at[kind, i],
            recv_sem=hop_recv.at[kind, i], device_id=twin, device_id_type=MESH,
        )

    own = m * rows
    own_basis.wait()
    for j in range(2):
        for way in range(2):
            @pl.when(gives(way, 0)[0])
            def _(way=way, j=j):
                along(way, 0, j).start()

    og_half = tokens // 2
    og_held, og_copies = [[q], [q]], [[], []]
    own_og.wait()
    for h in range(2):
        og_copies[h], og_held[h] = stage(og, 0, tokens, og_half, h, og_held[h], 0)
    twin_own = push(part(bas, own, rows), part(bas, own, rows), twin)

    def add(start):
        where = pl.multiple_of(start, 128)
        acc[...] += jnp.dot(
            act[:, pl.ds(where, rows)], bas[pl.ds(where, rows), :],
            preferred_element_type=jnp.float32,
        )

    acc[...] = jnp.zeros_like(acc)
    load_act.wait()
    add(own)

    def arrive(t):
        for j in range(2):
            for way in range(2):
                @pl.when(gets(way, t)[0])
                def _(way=way, j=j):
                    along_in(way, t, j).wait_recv()
                if t + 1 < chips - 1:
                    @pl.when(gives(way, t + 1)[0])
                    def _(way=way, j=j):
                        along(way, t + 1, j).start()
                @pl.when(gets(way, t)[0])
                def _(way=way, j=j):
                    across(way, t, j).start()
                    over(2, way, t, j).start()

    def settle(t):
        for way in range(2):
            @pl.when(gets(way, t)[0])
            def _(way=way):
                for j in range(2):
                    across_in(way, t, j).wait_recv()
                    over(3, way, t, j).start()
                add((2 * gets(way, t)[1] + c) * rows)

    arrive(0)
    for s in range(1, len(strides)):
        for h in range(2):
            for copy in og_copies[h]:
                copy.wait_recv()
            og_copies[h], og_held[h] = stage(og, 0, tokens, og_half, h, og_held[h], s)
    twin_own.wait_recv()
    add((2 * z + 1 - c) * rows)
    for t in range(1, chips - 1):
        arrive(t)
        settle(t - 1)
    settle(chips - 2)
    for t in range(chips - 1):
        for way in range(2):
            @pl.when(gets(way, t)[0])
            def _(way=way, t=t):
                for kind in (2, 3):
                    for j in range(2):
                        over_in(kind, way, t, j).wait_recv()
                add((2 * gets(way, t)[1] + 1 - c) * rows)

    place = q * tokens + m * mine
    red[pl.ds(pl.multiple_of(place, 16), mine), :] = acc[...].astype(red.dtype)
    group_copies = []
    for k in range(1, n_mp):
        where = part(red, place, mine)
        group_copies.append(push(where, where, (q, lax.rem(m + k, n_mp))))
    out_basis = pltpu.make_async_copy(bas, basis_out, local.at[2])
    out_basis.start()
    for copy in group_copies:
        copy.wait_recv()
    quarter = tokens // 4
    side = c * (tokens // 2)
    red_held, red_copies = [[q], [q]], [[], []]
    for s in range(len(strides)):
        for h in range(2):
            for copy in red_copies[h]:
                copy.wait_recv()
            red_copies[h], red_held[h] = stage(red, side, tokens, quarter, h, red_held[h], s)
    for h in range(2):
        for copy in red_copies[h]:
            copy.wait_recv()
    last = []
    for k in range(1, n_dp):
        where = part(red, lax.rem(q + k, n_dp) * tokens + side, tokens // 2)
        last.append(push(where, where, twin))
    for h in range(2):
        for copy in og_copies[h]:
            copy.wait_recv()
    out_og = pltpu.make_async_copy(og, og_out, local.at[3])
    out_og.start()
    for copy in last:
        copy.wait_recv()
    out_red = pltpu.make_async_copy(red, red_out, local.at[4])
    out_red.start()
    for copy in sent:
        copy.wait_send()
    for t in range(chips - 1):
        for way in range(2):
            @pl.when(gives(way, t)[0])
            def _(way=way, t=t):
                for j in range(2):
                    along(way, t, j).wait_send()
            @pl.when(gets(way, t)[0])
            def _(way=way, t=t):
                for j in range(2):
                    across(way, t, j).wait_send()
                    over(2, way, t, j).wait_send()
                    over(3, way, t, j).wait_send()
    out_basis.wait()
    out_og.wait()
    out_red.wait()


def gather(activations, out_grads, basis):
    n_dp, n_mp = lax.axis_size("dp"), lax.axis_size("mp")
    mine, width = activations.shape
    tokens, columns = out_grads.shape
    rank = basis.shape[1]
    hops, count = counts_of(n_dp, n_mp)
    anywhere = pl.BlockSpec(memory_space=pl.ANY)
    shapes = [(width, rank), (n_dp * tokens, columns), (n_dp * tokens, rank)]
    return pl.pallas_call(
        functools.partial(gather_kernel, n_dp, n_mp),
        out_shape=[jax.ShapeDtypeStruct(shape, jnp.bfloat16) for shape in shapes],
        in_specs=[anywhere] * 3,
        out_specs=[anywhere] * 3,
        scratch_shapes=[pltpu.VMEM(shape, jnp.bfloat16) for shape in [(mine, width)] + shapes]
        + [
            pltpu.VMEM((mine, rank), jnp.float32),
            pltpu.SemaphoreType.DMA((count,)),
            pltpu.SemaphoreType.DMA((count,)),
            pltpu.SemaphoreType.DMA((4, hops)),
            pltpu.SemaphoreType.DMA((4, hops)),
            pltpu.SemaphoreType.DMA((6,)),
        ],
        compiler_params=pltpu.CompilerParams(
            collective_id=0, has_side_effects=True, vmem_limit_bytes=58 * 2**20
        ),
        name="gather",
    )(activations, out_grads, basis)


def step_kernel(
    groups, blocks, basis_ref, red_ref, og_ref, first_ref, second_ref, update_ref, new_first_ref,
    new_second_ref, turned, normalized,
):
    i = pl.program_id(0)
    block = og_ref.shape[1]

    @pl.when(i == 0)
    def _():
        turned[...] = red_ref[...].T

    @pl.when(i < blocks)
    def _():
        projected = jnp.dot(turned[...], og_ref[...], preferred_element_type=jnp.float32) / groups
        new_first = 0.9 * first_ref[...] + 0.1 * projected
        new_second = 0.999 * second_ref[...] + 0.001 * projected * projected
        new_first_ref[...] = new_first
        new_second_ref[...] = new_second
        first_hat = new_first / (1.0 - 0.9**STEP)
        second_hat = new_second / (1.0 - 0.999**STEP)
        normalized[:, pl.ds(pl.multiple_of(i * block, block), block)] = (
            first_hat / (jnp.sqrt(second_hat) + 1e-08)
        ).astype(jnp.bfloat16)

    @pl.when(i >= blocks)
    def _():
        update_ref[...] = jnp.dot(
            basis_ref[...], normalized[...], preferred_element_type=jnp.float32
        ).astype(update_ref.dtype)


def step(basis, red, og, first, second, groups):
    rank, columns = first.shape
    width, tokens = basis.shape[0], og.shape[0]
    block = next(b for b in (columns // 2, 256, 128) if b % 128 == 0 and columns % b == 0)
    blocks = columns // block
    high = min(width, 1024)
    row = lambda n: pl.BlockSpec((high, n), lambda i: (jnp.maximum(i - blocks, 0), 0))
    column = lambda n: pl.BlockSpec((n, block), lambda i: (0, jnp.minimum(i, blocks - 1)))
    return pl.pallas_call(
        functools.partial(step_kernel, groups, blocks),
        grid=(blocks + width // high,),
        out_shape=[
            jax.ShapeDtypeStruct((width, columns), jnp.bfloat16),
            jax.ShapeDtypeStruct(first.shape, jnp.float32),
            jax.ShapeDtypeStruct(second.shape, jnp.float32),
        ],
        in_specs=[
            row(rank),
            pl.BlockSpec((tokens, rank), lambda i: (0, 0), pipeline_mode=pl.Buffered(1)),
            column(tokens), column(rank), column(rank),
        ],
        out_specs=[row(columns), column(rank), column(rank)],
        scratch_shapes=[
            pltpu.VMEM((rank, tokens), jnp.bfloat16), pltpu.VMEM((rank, columns), jnp.bfloat16)
        ],
        compiler_params=pltpu.CompilerParams(vmem_limit_bytes=48 * 2**20),
        name="step",
    )(basis, red, og, first, second)


def body(activations, out_grads, basis, first_moment, second_moment):
    whole_basis, whole_grads, reduced = gather(activations, out_grads, basis)
    return tuple(step(
        whole_basis, reduced, whole_grads, first_moment, second_moment, lax.axis_size("dp")
    ))


def solution(mesh):
    return jax.shard_map(
        body,
        mesh=mesh,
        in_specs=(
            P(("dp", "mp"), None),
            P("dp", "mp"),
            P("mp", None),
            P(None, "mp"),
            P(None, "mp"),
        ),
        out_specs=(P(None, "mp"), P(None, "mp"), P(None, "mp")),
        check_vma=False,
    )
```

```python
import functools
import itertools

import jax
import jax.numpy as jnp
from jax import lax
from jax.experimental import pallas as pl
from jax.experimental.pallas import tpu as pltpu
from jax.sharding import PartitionSpec as P

STEP = 10
MESH = pl.DeviceIdType.MESH


def flip(index, stride):
    return index + stride - 2 * stride * lax.rem(lax.div(index, stride), 2)


def counts_of(n_dp, n_mp):
    hops = 4 * (n_mp // 2 - 1)
    both = 2 * (n_dp - 1)
    return hops, 1 + both + (n_mp - 1) + both + (n_dp - 1)


def gather_kernel(
    n_dp, n_mp, act_ref, og_ref, basis_ref, basis_out, og_out, red_out,
    act, bas, og, red, acc, send, recv, hop_send, hop_recv, local,
):
    q, m = lax.axis_index("dp"), lax.axis_index("mp")
    chips = n_mp // 2
    z, c = lax.div(m, 2), lax.rem(m, 2)
    twin = (q, 2 * z + 1 - c)
    strides = [1 << s for s in range(n_dp.bit_length() - 1)]
    orders = [strides, strides[::-1]]
    rows = basis_ref.shape[0]
    piece = rows // 4
    tokens = og_ref.shape[0]
    mine = act_ref.shape[0]

    load_act = pltpu.make_async_copy(act_ref, act, local.at[5])
    load_act.start()
    own_basis = pltpu.make_async_copy(basis_ref, bas.at[pl.ds(pl.multiple_of(m * rows, 128), rows), :], local.at[0])
    own_basis.start()
    own_og = pltpu.make_async_copy(og_ref, og.at[pl.ds(pl.multiple_of(q * tokens, 128), tokens), :], local.at[1])
    own_og.start()

    barrier = pltpu.get_barrier_semaphore()
    for k in range(1, n_mp):
        pl.semaphore_signal(barrier, inc=1, device_id=(q, lax.rem(m + k, n_mp)), device_id_type=MESH)
    for stride in strides:
        pl.semaphore_signal(barrier, inc=1, device_id=(flip(q, stride), m), device_id_type=MESH)
    pl.semaphore_wait(barrier, n_mp - 1 + len(strides))

    numbers = itertools.count()
    sent = []

    def push(src, dst, device):
        i = next(numbers)
        copy = pltpu.make_async_remote_copy(
            src_ref=src, dst_ref=dst, send_sem=send.at[i], recv_sem=recv.at[i],
            device_id=device, device_id_type=MESH,
        )
        copy.start()
        sent.append(copy)
        return copy

    def part(ref, start, size):
        return ref.at[pl.ds(pl.multiple_of(start, 16), size), :]

    def stage(ref, base, step, size, half, held, s):
        stride = orders[half][s]
        partner = (flip(q, stride), m)
        copies = []
        for b in held:
            where = part(ref, base + b * step + half * size, size)
            copies.append(push(where, where, partner))
        return copies, held + [flip(b, stride) for b in held]

    parity = lax.rem(lax.rem(q, 2) + lax.rem(lax.div(q, 2), 2), 2)
    neighbours = [(flip(q, 1), m), (flip(q, 2), m)]
    ways = [1, -1]

    def hop(kind, way, t, j, shard_z, half_number, device):
        i = (way * (chips - 1) + t) * 2 + j
        where = part(bas, (2 * shard_z + c) * rows + half_number * 2 * piece + j * piece, piece)
        return pltpu.make_async_remote_copy(
            src_ref=where, dst_ref=where, send_sem=hop_send.at[kind, i],
            recv_sem=hop_recv.at[kind, i], device_id=device, device_id_type=MESH,
        )

    def gives(way, t):
        if way == 0:
            return jnp.logical_and(z < chips - 1, z - t >= 0), z - t
        return jnp.logical_and(z > 0, z + t <= chips - 1), z + t

    def gets(way, t):
        if way == 0:
            return z - 1 - t >= 0, z - 1 - t
        return z + 1 + t <= chips - 1, z + 1 + t

    def along(way, t, j):
        return hop(0, way, t, j, gives(way, t)[1], parity, (q, m + 2 * ways[way]))

    def along_in(way, t, j):
        return hop(0, way, t, j, gets(way, t)[1], parity, (q, m - 2 * ways[way]))

    def across(way, t, j):
        return hop(1, way, t, j, gets(way, t)[1], parity, neighbours[j])

    def across_in(way, t, j):
        return hop(1, way, t, j, gets(way, t)[1], 1 - parity, neighbours[j])

    def over(kind, way, t, j):
        half_number = parity if kind == 2 else 1 - parity
        return hop(kind, way, t, j, gets(way, t)[1], half_number, twin)

    def over_in(kind, way, t, j):
        half_number = parity if kind == 2 else 1 - parity
        i = (way * (chips - 1) + t) * 2 + j
        start = (2 * gets(way, t)[1] + 1 - c) * rows + half_number * 2 * piece + j * piece
        where = part(bas, start, piece)
        return pltpu.make_async_remote_copy(
            src_ref=where, dst_ref=where, send_sem=hop_send.at[kind, i],
            recv_sem=hop_recv.at[kind, i], device_id=twin, device_id_type=MESH,
        )

    own = m * rows
    own_basis.wait()
    for j in range(2):
        for way in range(2):
            @pl.when(gives(way, 0)[0])
            def _(way=way, j=j):
                along(way, 0, j).start()

    og_half = tokens // 2
    og_held, og_copies = [[q], [q]], [[], []]
    own_og.wait()
    for h in range(2):
        og_copies[h], og_held[h] = stage(og, 0, tokens, og_half, h, og_held[h], 0)
    twin_own = push(part(bas, own, rows), part(bas, own, rows), twin)

    def add(start):
        where = pl.multiple_of(start, 128)
        acc[...] += jnp.dot(
            act[:, pl.ds(where, rows)], bas[pl.ds(where, rows), :],
            preferred_element_type=jnp.float32,
        )

    acc[...] = jnp.zeros_like(acc)
    load_act.wait()
    add(own)

    def arrive(t):
        for j in range(2):
            for way in range(2):
                @pl.when(gets(way, t)[0])
                def _(way=way, j=j):
                    along_in(way, t, j).wait_recv()
                if t + 1 < chips - 1:
                    @pl.when(gives(way, t + 1)[0])
                    def _(way=way, j=j):
                        along(way, t + 1, j).start()
                @pl.when(gets(way, t)[0])
                def _(way=way, j=j):
                    across(way, t, j).start()
                    over(2, way, t, j).start()

    def settle(t):
        for way in range(2):
            @pl.when(gets(way, t)[0])
            def _(way=way):
                for j in range(2):
                    across_in(way, t, j).wait_recv()
                    over(3, way, t, j).start()
                add((2 * gets(way, t)[1] + c) * rows)

    arrive(0)
    for s in range(1, len(strides)):
        for h in (0,):
            for copy in og_copies[h]:
                copy.wait_recv()
            og_copies[h], og_held[h] = stage(og, 0, tokens, og_half, h, og_held[h], s)
    twin_own.wait_recv()
    add((2 * z + 1 - c) * rows)
    for t in range(1, chips - 1):
        arrive(t)
        settle(t - 1)
    settle(chips - 2)
    for s in range(1, len(strides)):
        for h in (1,):
            for copy in og_copies[h]:
                copy.wait_recv()
            og_copies[h], og_held[h] = stage(og, 0, tokens, og_half, h, og_held[h], s)
    for t in range(chips - 1):
        for way in range(2):
            @pl.when(gets(way, t)[0])
            def _(way=way, t=t):
                for kind in (2, 3):
                    for j in range(2):
                        over_in(kind, way, t, j).wait_recv()
                add((2 * gets(way, t)[1] + 1 - c) * rows)

    place = q * tokens + m * mine
    red[pl.ds(pl.multiple_of(place, 16), mine), :] = acc[...].astype(red.dtype)
    group_copies = []
    for k in range(1, n_mp):
        where = part(red, place, mine)
        group_copies.append(push(where, where, (q, lax.rem(m + k, n_mp))))
    out_basis = pltpu.make_async_copy(bas, basis_out, local.at[2])
    out_basis.start()
    for copy in group_copies:
        copy.wait_recv()
    quarter = tokens // 4
    side = c * (tokens // 2)
    red_held, red_copies = [[q], [q]], [[], []]
    for s in range(len(strides)):
        for h in range(2):
            for copy in red_copies[h]:
                copy.wait_recv()
            red_copies[h], red_held[h] = stage(red, side, tokens, quarter, h, red_held[h], s)
    for h in range(2):
        for copy in red_copies[h]:
            copy.wait_recv()
    last = []
    for k in range(1, n_dp):
        where = part(red, lax.rem(q + k, n_dp) * tokens + side, tokens // 2)
        last.append(push(where, where, twin))
    for h in range(2):
        for copy in og_copies[h]:
            copy.wait_recv()
    out_og = pltpu.make_async_copy(og, og_out, local.at[3])
    out_og.start()
    for copy in last:
        copy.wait_recv()
    out_red = pltpu.make_async_copy(red, red_out, local.at[4])
    out_red.start()
    for copy in sent:
        copy.wait_send()
    for t in range(chips - 1):
        for way in range(2):
            @pl.when(gives(way, t)[0])
            def _(way=way, t=t):
                for j in range(2):
                    along(way, t, j).wait_send()
            @pl.when(gets(way, t)[0])
            def _(way=way, t=t):
                for j in range(2):
                    across(way, t, j).wait_send()
                    over(2, way, t, j).wait_send()
                    over(3, way, t, j).wait_send()
    out_basis.wait()
    out_og.wait()
    out_red.wait()


def gather(activations, out_grads, basis):
    n_dp, n_mp = lax.axis_size("dp"), lax.axis_size("mp")
    mine, width = activations.shape
    tokens, columns = out_grads.shape
    rank = basis.shape[1]
    hops, count = counts_of(n_dp, n_mp)
    anywhere = pl.BlockSpec(memory_space=pl.ANY)
    shapes = [(width, rank), (n_dp * tokens, columns), (n_dp * tokens, rank)]
    return pl.pallas_call(
        functools.partial(gather_kernel, n_dp, n_mp),
        out_shape=[jax.ShapeDtypeStruct(shape, jnp.bfloat16) for shape in shapes],
        in_specs=[anywhere] * 3,
        out_specs=[anywhere] * 3,
        scratch_shapes=[pltpu.VMEM(shape, jnp.bfloat16) for shape in [(mine, width)] + shapes]
        + [
            pltpu.VMEM((mine, rank), jnp.float32),
            pltpu.SemaphoreType.DMA((count,)),
            pltpu.SemaphoreType.DMA((count,)),
            pltpu.SemaphoreType.DMA((4, hops)),
            pltpu.SemaphoreType.DMA((4, hops)),
            pltpu.SemaphoreType.DMA((6,)),
        ],
        compiler_params=pltpu.CompilerParams(
            collective_id=0, has_side_effects=True, vmem_limit_bytes=58 * 2**20
        ),
        name="gather",
    )(activations, out_grads, basis)


def step_kernel(
    groups, blocks, basis_ref, red_ref, og_ref, first_ref, second_ref, update_ref, new_first_ref,
    new_second_ref, turned, normalized,
):
    i = pl.program_id(0)
    block = og_ref.shape[1]

    @pl.when(i == 0)
    def _():
        turned[...] = red_ref[...].T

    @pl.when(i < blocks)
    def _():
        projected = jnp.dot(turned[...], og_ref[...], preferred_element_type=jnp.float32) / groups
        new_first = 0.9 * first_ref[...] + 0.1 * projected
        new_second = 0.999 * second_ref[...] + 0.001 * projected * projected
        new_first_ref[...] = new_first
        new_second_ref[...] = new_second
        first_hat = new_first / (1.0 - 0.9**STEP)
        second_hat = new_second / (1.0 - 0.999**STEP)
        normalized[:, pl.ds(pl.multiple_of(i * block, block), block)] = (
            first_hat / (jnp.sqrt(second_hat) + 1e-08)
        ).astype(jnp.bfloat16)

    @pl.when(i >= blocks)
    def _():
        update_ref[...] = jnp.dot(
            basis_ref[...], normalized[...], preferred_element_type=jnp.float32
        ).astype(update_ref.dtype)


def step(basis, red, og, first, second, groups):
    rank, columns = first.shape
    width, tokens = basis.shape[0], og.shape[0]
    block = next(b for b in (columns // 2, 256, 128) if b % 128 == 0 and columns % b == 0)
    blocks = columns // block
    high = min(width, 1024)
    row = lambda n: pl.BlockSpec((high, n), lambda i: (jnp.maximum(i - blocks, 0), 0))
    column = lambda n: pl.BlockSpec((n, block), lambda i: (0, jnp.minimum(i, blocks - 1)))
    return pl.pallas_call(
        functools.partial(step_kernel, groups, blocks),
        grid=(blocks + width // high,),
        out_shape=[
            jax.ShapeDtypeStruct((width, columns), jnp.bfloat16),
            jax.ShapeDtypeStruct(first.shape, jnp.float32),
            jax.ShapeDtypeStruct(second.shape, jnp.float32),
        ],
        in_specs=[
            row(rank),
            pl.BlockSpec((tokens, rank), lambda i: (0, 0), pipeline_mode=pl.Buffered(1)),
            column(tokens), column(rank), column(rank),
        ],
        out_specs=[row(columns), column(rank), column(rank)],
        scratch_shapes=[
            pltpu.VMEM((rank, tokens), jnp.bfloat16), pltpu.VMEM((rank, columns), jnp.bfloat16)
        ],
        compiler_params=pltpu.CompilerParams(vmem_limit_bytes=60 * 2**20),
        name="step",
    )(basis, red, og, first, second)


def body(activations, out_grads, basis, first_moment, second_moment):
    whole_basis, whole_grads, reduced = gather(activations, out_grads, basis)
    return tuple(step(
        whole_basis, reduced, whole_grads, first_moment, second_moment, lax.axis_size("dp")
    ))


def solution(mesh):
    return jax.shard_map(
        body,
        mesh=mesh,
        in_specs=(
            P(("dp", "mp"), None),
            P("dp", "mp"),
            P("mp", None),
            P(None, "mp"),
            P(None, "mp"),
        ),
        out_specs=(P(None, "mp"), P(None, "mp"), P(None, "mp")),
        check_vma=False,
    )
```
